32 devices in a mesh: mem: 4 (over y, x), col: 8 (over z, core).
Axes of the slice: x: 2, y: 2, z: 4, core: 2. Of those that a mesh axis runs over, the one named last changes fastest.
Arguments:
- prior: float32 [80, 32, 24576], P('mem', 'col'), may hold values from -6 to 6
- obs_column: int32 [2, 512], replicated, may hold values from 0 to 24575, as said below
- obs_level: int32 [2, 512], replicated, may hold values from 0 to 31
- obs_value: float32 [2, 512], replicated, may hold values from -8 to 8
- obs_variance: float32 [2, 512], replicated, may hold values from 0.3 to 3
Outputs:
- analysis: float32 [80, 32, 24576], P('mem', 'col')
The draws below stay inside these ranges and needn't reach their ends.
Inputs may be any that keep to these rules, and one draw needn't show every extreme that they name: `obs_column`: each batch (row) is sorted in non-decreasing order; the first observation of every batch lies at column 0 and the last at column 24575; several observations may share a column.
All inputs are finite; a program needn't handle non-finite values.
Results may differ from the reference program's by a relative error of at most 0.0001.
Values sent between devices are 32-bit elements; how exact they have to be, the bound alone decides.
A program may use at most 192 MiB of HBM per device.

```python
import math
import jax
import jax.numpy as jnp
from jax import lax

K = 80
LEVELS = 16
VARS = 2
NLON = 768
P_SIZE = 512
NB = 2
LOCR = 6
NLAT = 32
NCOL = 24576


def draw_obs_column(key, part):
    key = jax.random.fold_in(key, 11)
    keys = jax.random.split(key, 7)
    centers = jax.random.randint(keys[0], (NB, 3), 0, NLAT)
    choice_idx = jax.random.randint(keys[1], (NB, P_SIZE), 0, 3)
    center_row = jnp.take_along_axis(centers, choice_idx, axis=1)
    spread_rows = max(NLAT // 16, 1)
    offset = jax.random.randint(keys[2], (NB, P_SIZE), -spread_rows, spread_rows + 1)
    offset = offset + jax.random.randint(keys[3], (NB, P_SIZE), -spread_rows, spread_rows + 1)
    dense_row = jnp.clip(center_row + offset, 0, NLAT - 1)
    even_row = jax.random.randint(keys[4], (NB, P_SIZE), 0, NLAT)
    pick_dense = jax.random.randint(keys[5], (NB, P_SIZE), 0, 10) < 6
    lat_row = jnp.where(pick_dense, dense_row, even_row)
    longitude = jax.random.randint(keys[6], (NB, P_SIZE), 0, NLON)
    columns = lat_row * NLON + longitude
    columns = columns.at[:, 0].set(0)
    columns = columns.at[:, P_SIZE - 1].set(NCOL - 1)
    return jnp.sort(columns, axis=1).astype(jnp.int32)


def with_ends(array, key, least, high):
    longest = array.shape.index(max(array.shape))
    spots = []
    for shift in (0, 1):
        where = [jax.random.randint(jax.random.fold_in(key, axis), (), 0, length) for axis, length in enumerate(array.shape)]
        where[longest] = (where[longest] + shift) % array.shape[longest]
        spots.append(tuple(where))
    return array.at[spots[0]].set(least).at[spots[1]].set(high)


def levels(key, shape, shards, least, top_value):
    def one(axis_at, parts):
        draws = jax.random.uniform(jax.random.fold_in(jax.random.fold_in(key, 6), axis_at), (parts,), jnp.float32, least / len(shards), top_value / len(shards))
        return jnp.repeat(jnp.exp(draws), shape[axis_at] // parts).reshape((-1,) + (1,) * (len(shape) - axis_at - 1))

    factor_of = one(*shards[0])
    for cut in shards[1:]:
        factor_of = factor_of * one(*cut)
    return factor_of


def centred(rng, shape, scale, most, pieces=(), kind=jnp.bfloat16):
    loudness = levels(rng, shape, pieces, -0.22, 0.18) if pieces else 1.0
    values = jax.random.normal(rng, shape, jnp.float32) * scale * loudness
    return jnp.minimum(jnp.maximum(values, -most), most).astype(kind)


def setup_inputs(seed: int = 0) -> dict:
    streams_of = jax.random.split(jax.random.key(seed), 6)
    prior = centred(streams_of[0], (K, LEVELS * VARS, NCOL), 1.0, 6.0, ((0, 4), (1, 8)), jnp.float32)
    obs_column = draw_obs_column(jax.random.fold_in(streams_of[5], 71), 0)
    obs_level = with_ends(jax.random.randint(streams_of[2], (NB, P_SIZE), 0, LEVELS * VARS), jax.random.fold_in(streams_of[2], 1), 0, (LEVELS * VARS) - 1).astype(jnp.int32)
    obs_value = centred(streams_of[3], (NB, P_SIZE), 1.5, 8.0, (), jnp.float32)
    obs_variance = jnp.clip(jnp.exp(jax.random.uniform(streams_of[4], (NB, P_SIZE), jnp.float32, math.log(0.3), math.log(3.0))), 0.3, 3.0)
    return {"prior": prior, "obs_column": obs_column, "obs_level": obs_level, "obs_value": obs_value, "obs_variance": obs_variance}


def gc_taper(squared_gap, radius):
    scaled = jnp.sqrt(squared_gap.astype(jnp.float32)) / radius
    near_part = (((-0.25 * scaled + 0.5) * scaled + 0.625) * scaled - 5.0 / 3.0) * scaled * scaled + 1.0
    bounded = jnp.maximum(scaled, 1.0)
    far_part = ((((scaled / 12.0 - 0.5) * scaled + 0.625) * scaled + 5.0 / 3.0) * scaled - 5.0) * scaled + 4.0 - 2.0 / (3.0 * bounded)
    zero_part = jnp.zeros_like(scaled)
    result = jnp.where(squared_gap < radius * radius, near_part, jnp.where(squared_gap < 4 * radius * radius, far_part, zero_part))
    return result.astype(jnp.float32)

def localize(obs_cols, first_col, count):
    col_index = first_col + jnp.arange(count, dtype=jnp.int32)
    row_gap = col_index[None, :] // NLON - obs_cols[:, None] // NLON
    lon_gap = jnp.abs(col_index[None, :] % NLON - obs_cols[:, None] % NLON)
    lon_gap = jnp.minimum(lon_gap, NLON - lon_gap)
    return gc_taper(row_gap * row_gap + lon_gap * lon_gap, LOCR)

def obs_weights(picked, values, variances):
    obs_mean = lax.optimization_barrier(jnp.mean(picked, axis=0))
    obs_anom = picked - obs_mean[None, :]
    obs_total = lax.optimization_barrier(jnp.sum(obs_anom * obs_anom, axis=0)) / (K - 1) + variances
    mean_gain = (values - obs_mean) / obs_total
    root_gain = 1.0 / (obs_total * (1.0 + jnp.sqrt(variances / obs_total)))
    weights = mean_gain[None, :] - root_gain[None, :] * obs_anom
    return (obs_anom, weights)

def reference(prior, obs_column, obs_level, obs_value, obs_variance):
    field_state = prior
    for batch_index in range(NB):
        flattened = field_state.reshape(K, LEVELS * VARS * NCOL)
        position = (obs_level[batch_index] * NCOL + obs_column[batch_index]).astype(jnp.int32)
        picked = jnp.take(flattened, position, axis=1)
        obs_anom, weights = obs_weights(picked, obs_value[batch_index], obs_variance[batch_index])
        field_mean = lax.optimization_barrier(jnp.mean(field_state, axis=0))
        columns = obs_column[batch_index]
        start_state = field_state

        def row_step(row_index, updated):
            first_col = (row_index * NLON).astype(jnp.int32)
            slab = lax.dynamic_slice_in_dim(start_state, first_col, NLON, 2)
            slab = slab - lax.dynamic_slice_in_dim(field_mean, first_col, NLON, 1)[None]
            covariance = jnp.einsum('kp,klc->plc', obs_anom, slab, precision=lax.Precision.HIGHEST, preferred_element_type=jnp.float32) / (K - 1)
            gain_block = covariance * localize(columns, first_col, NLON)[:, None, :]
            increment = jnp.einsum('kp,plc->klc', weights, gain_block, precision=lax.Precision.HIGHEST, preferred_element_type=jnp.float32)
            previous = lax.dynamic_slice_in_dim(updated, first_col, NLON, 2)
            return lax.dynamic_update_slice_in_dim(updated, previous + increment, first_col, 2)
        field_state = lax.fori_loop(0, NLAT, row_step, start_state)
    return field_state
```

```python
import functools

import jax
import jax.numpy as jnp
from jax import lax
from jax.experimental import pallas as pl
from jax.experimental.pallas import tpu as pltpu
from jax.sharding import PartitionSpec as P

NLON = 768
P_SIZE = 512
NB = 2
LOCR = 6
REACH = 2 * LOCR
LANES = 128
BLOCKS = NLON // LANES
CHUNK = 80
CHUNKS = -(-P_SIZE // CHUNK)
PADDED = CHUNK * CHUNKS
SLABS = 4
GROUP = 4
MESH = pl.DeviceIdType.MESH


def gc_taper(squared_gap):
    scaled = jnp.sqrt(squared_gap) * (1.0 / LOCR)
    near_part = (
        ((-0.25 * scaled + 0.5) * scaled + 0.625) * scaled - 5.0 / 3.0
    ) * scaled * scaled + 1.0
    bounded = jnp.maximum(scaled, 1.0)
    far_part = (
        ((((scaled / 12.0 - 0.5) * scaled + 0.625) * scaled + 5.0 / 3.0) * scaled - 5.0) * scaled
        + 4.0
        - 2.0 / (3.0 * bounded)
    )
    return jnp.where(
        squared_gap < LOCR * LOCR,
        near_part,
        jnp.where(squared_gap < 4 * LOCR * LOCR, far_part, 0.0),
    )


def taper_of(rows, lons, obs_rows, obs_lons):
    row_gap = rows - obs_rows
    lon_gap = jnp.abs(lons - obs_lons)
    lon_gap = jnp.minimum(lon_gap, NLON - lon_gap)
    return gc_taper(row_gap * row_gap + lon_gap * lon_gap)


def obs_weights(picked, values, variances):
    members = picked.shape[0]
    obs_mean = jnp.mean(picked, axis=0)
    obs_anom = picked - obs_mean[None, :]
    obs_total = jnp.sum(obs_anom * obs_anom, axis=0) / (members - 1) + variances
    mean_gain = (values - obs_mean) / obs_total
    root_gain = 1.0 / (obs_total * (1.0 + jnp.sqrt(variances / obs_total)))
    weights = mean_gain[None, :] - root_gain[None, :] * obs_anom
    return (obs_anom, weights)


def split(x):
    high = x.astype(jnp.bfloat16)
    low = (x - high.astype(jnp.float32)).astype(jnp.bfloat16)
    return high, low


def split_outside(x):
    high = lax.reduce_precision(x, exponent_bits=8, mantissa_bits=7)
    return high.astype(jnp.bfloat16), (x - high).astype(jnp.bfloat16)


def exchange_in_kernel(mem_n, col_n, prior, picked, tile, obs, slots, total, sends, recvs, own, psend, precv, osend, orecv):
    m = lax.axis_index("mem")
    c = lax.axis_index("col")
    rows = prior.shape[1]
    tiles = tile.shape[0]
    here = pl.ds(pl.multiple_of(m * rows, 8), rows)
    barrier = pltpu.get_barrier_semaphore()
    for j in range(1, mem_n):
        pl.semaphore_signal(barrier, inc=1, device_id=(lax.rem(m + j, mem_n), c), device_id_type=MESH)
    for j in range(1, col_n):
        pl.semaphore_signal(barrier, inc=1, device_id=(m, lax.rem(c + j, col_n)), device_id_type=MESH)
    pl.semaphore_wait(barrier, mem_n + col_n - 2)

    picks = []
    for j in range(1, col_n):
        copy = pltpu.make_async_remote_copy(
            src_ref=picked,
            dst_ref=slots.at[j],
            send_sem=psend.at[j],
            recv_sem=precv.at[j],
            device_id=(m, lax.rem(c + j, col_n)),
            device_id_type=MESH,
        )
        copy.start()
        picks.append(copy)
    bulk = []
    for j in range(1, mem_n):
        q = lax.rem(m + j, mem_n)
        copy = pltpu.make_async_remote_copy(
            src_ref=prior.at[pl.ds(q * tiles, tiles)],
            dst_ref=tile.at[:, here],
            send_sem=sends.at[j],
            recv_sem=recvs.at[j],
            device_id=(q, c),
            device_id_type=MESH,
        )
        copy.start()
        bulk.append(copy)
    mine = pltpu.make_async_copy(prior.at[pl.ds(m * tiles, tiles)], tile.at[:, here], own)
    mine.start()
    for copy in picks:
        copy.wait_recv()
    summed = picked[...]
    for j in range(1, col_n):
        summed = summed + slots[j]
    total[...] = summed
    obs[m] = summed
    shares = []
    for j in range(1, mem_n):
        copy = pltpu.make_async_remote_copy(
            src_ref=total,
            dst_ref=obs.at[m],
            send_sem=osend.at[j],
            recv_sem=orecv.at[j],
            device_id=(lax.rem(m + j, mem_n), c),
            device_id_type=MESH,
        )
        copy.start()
        shares.append(copy)
    for copy in shares:
        copy.wait()
    for copy in picks:
        copy.wait_send()
    for copy in bulk:
        copy.wait()
    mine.wait()


def exchange_in(prior, picked, mem_n, col_n):
    tiles, rows, lanes = prior.shape
    return pl.pallas_call(
        functools.partial(exchange_in_kernel, mem_n, col_n),
        out_shape=(
            jax.ShapeDtypeStruct((tiles // mem_n, rows * mem_n, lanes), jnp.float32),
            jax.ShapeDtypeStruct((mem_n,) + picked.shape, jnp.float32),
        ),
        in_specs=[pl.BlockSpec(memory_space=pl.ANY), pl.BlockSpec(memory_space=pltpu.VMEM)],
        out_specs=(pl.BlockSpec(memory_space=pl.ANY), pl.BlockSpec(memory_space=pltpu.VMEM)),
        scratch_shapes=[
            pltpu.VMEM((col_n,) + picked.shape, jnp.float32),
            pltpu.VMEM(picked.shape, jnp.float32),
            pltpu.SemaphoreType.DMA((mem_n,)),
            pltpu.SemaphoreType.DMA((mem_n,)),
            pltpu.SemaphoreType.DMA,
            pltpu.SemaphoreType.DMA((col_n,)),
            pltpu.SemaphoreType.DMA((col_n,)),
            pltpu.SemaphoreType.DMA((mem_n,)),
            pltpu.SemaphoreType.DMA((mem_n,)),
        ],
        compiler_params=pltpu.CompilerParams(collective_id=0, has_side_effects=True),
        name="exchange_in",
    )(prior, picked)


def exchange_out_kernel(mem_n, tile, out, sends, recvs, own):
    m = lax.axis_index("mem")
    c = lax.axis_index("col")
    rows = out.shape[1]
    tiles = tile.shape[0]
    barrier = pltpu.get_barrier_semaphore()
    for j in range(1, mem_n):
        pl.semaphore_signal(barrier, inc=1, device_id=(lax.rem(m + j, mem_n), c), device_id_type=MESH)
    pl.semaphore_wait(barrier, mem_n - 1)
    bulk = []
    place = pl.ds(m * tiles, tiles)
    for j in range(1, mem_n):
        q = lax.rem(m + j, mem_n)
        copy = pltpu.make_async_remote_copy(
            src_ref=tile.at[:, pl.ds(pl.multiple_of(q * rows, 8), rows)],
            dst_ref=out.at[place],
            send_sem=sends.at[j],
            recv_sem=recvs.at[j],
            device_id=(q, c),
            device_id_type=MESH,
        )
        copy.start()
        bulk.append(copy)
    mine = pltpu.make_async_copy(
        tile.at[:, pl.ds(pl.multiple_of(m * rows, 8), rows)], out.at[place], own
    )
    mine.start()
    for copy in bulk:
        copy.wait()
    mine.wait()


def exchange_out(tile, mem_n):
    tiles, all_rows, lanes = tile.shape
    return pl.pallas_call(
        functools.partial(exchange_out_kernel, mem_n),
        out_shape=jax.ShapeDtypeStruct((tiles * mem_n, all_rows // mem_n, lanes), jnp.float32),
        in_specs=[pl.BlockSpec(memory_space=pl.ANY)],
        out_specs=pl.BlockSpec(memory_space=pl.ANY),
        scratch_shapes=[
            pltpu.SemaphoreType.DMA((mem_n,)),
            pltpu.SemaphoreType.DMA((mem_n,)),
            pltpu.SemaphoreType.DMA,
        ],
        compiler_params=pltpu.CompilerParams(collective_id=1, has_side_effects=True),
        name="exchange_out",
    )(tile)


def update_kernel(members, shared, near, first_row, tile, anom, weight, obs_row, obs_lon, out, current, spread):
    groups = tile.shape[0] // (BLOCKS * GROUP)
    span = GROUP * LANES
    lane = lax.broadcasted_iota(jnp.int32, (1, LANES), 1)

    def step(index, carry):
        block = index // groups
        group = lax.rem(index, groups)
        starts = [(group * GROUP + r) * BLOCKS + block for r in range(GROUP)]
        for s in range(SLABS):
            for r in range(GROUP):
                at = s * span + r * LANES
                current[:, at : at + LANES] = tile[starts[r], pl.ds(s, members, stride=SLABS), :]
        lons = (block * LANES + lane).astype(jnp.float32)
        for b in range(NB):
            for s in range(SLABS):
                part = current[:, s * span : (s + 1) * span]
                high, low = split(part - jnp.mean(part, axis=0, keepdims=True))
                spread[:, s * span : (s + 1) * span] = jnp.concatenate([high, low, high], axis=0)
            for chunk in range(CHUNKS):

                @pl.when(near[b, chunk, block] != 0)
                def _():
                    here = pl.ds(chunk * CHUNK, CHUNK)
                    rows_here = obs_row[b, here, :]
                    lons_here = obs_lon[b, here, :]
                    gains = None
                    for s in range(SLABS):
                        if s == 0 or not shared:
                            gains = jnp.concatenate(
                                [
                                    taper_of(
                                        (first_row[s] + group * GROUP + r).astype(jnp.float32),
                                        lons,
                                        rows_here,
                                        lons_here,
                                    )
                                    for r in range(GROUP)
                                ],
                                axis=1,
                            )
                        cov = jnp.dot(
                            anom[b, here, :],
                            spread[:, s * span : (s + 1) * span],
                            preferred_element_type=jnp.float32,
                        )
                        high, low = split(cov * gains)
                        current[:, s * span : (s + 1) * span] += jnp.dot(
                            weight[b, chunk],
                            jnp.concatenate([high, low, high], axis=0),
                            preferred_element_type=jnp.float32,
                        )
        for s in range(SLABS):
            for r in range(GROUP):
                at = s * span + r * LANES
                out[starts[r], pl.ds(s, members, stride=SLABS), :] = current[:, at : at + LANES]
        return carry

    lax.fori_loop(0, BLOCKS * groups, step, 0)


def update(tile, near, first_row, anom, weight, obs_row, obs_lon, shared):
    members = tile.shape[1] // SLABS
    whole = pl.BlockSpec(memory_space=pltpu.VMEM)
    scalars = pl.BlockSpec(memory_space=pltpu.SMEM)
    return pl.pallas_call(
        functools.partial(update_kernel, members, shared),
        out_shape=jax.ShapeDtypeStruct(tile.shape, jnp.float32),
        in_specs=[scalars, scalars, whole, whole, whole, whole, whole],
        out_specs=whole,
        scratch_shapes=[
            pltpu.VMEM((members, SLABS * GROUP * LANES), jnp.float32),
            pltpu.VMEM((3 * members, SLABS * GROUP * LANES), jnp.bfloat16),
        ],
        compiler_params=pltpu.CompilerParams(vmem_limit_bytes=40 * 1024 * 1024),
        name="update",
    )(near, first_row, tile, anom, weight, obs_row, obs_lon)


def by_longitude(columns, arrays):
    lons = columns % NLON
    count = columns.shape[1]
    index = jnp.arange(count, dtype=jnp.int32)
    before = (lons[:, :, None] < lons[:, None, :]) | (
        (lons[:, :, None] == lons[:, None, :]) & (index[:, None] < index[None, :])[None]
    )
    rank = jnp.sum(before.astype(jnp.int32), axis=1)
    chosen = rank[:, :, None] == index[None, None, :]
    return [jnp.sum(jnp.where(chosen, a[:, :, None], jnp.zeros((), a.dtype)), axis=1) for a in arrays]


def near_blocks(columns):
    lons = columns % NLON
    past = (lons[:, :, None] - (jnp.arange(BLOCKS, dtype=jnp.int32) * LANES)[None, None, :]) % NLON
    hit = (past < LANES + REACH) | (past > NLON - REACH)
    hit = jnp.pad(hit, ((0, 0), (0, PADDED - P_SIZE), (0, 0)))
    return jnp.any(hit.reshape(NB, CHUNKS, CHUNK, BLOCKS), axis=2).astype(jnp.int32)


def local(prior, obs_column, obs_level, obs_value, obs_variance):
    own_members, own_levels, all_columns = prior.shape
    mem_n = lax.axis_size("mem")
    col_n = lax.axis_size("col")
    m = lax.axis_index("mem")
    c = lax.axis_index("col")
    members = own_members * mem_n
    parts = SLABS // own_levels
    part_columns = all_columns // parts
    width = part_columns // mem_n
    tiles = part_columns // LANES
    prior = prior.reshape(own_members, SLABS, part_columns)

    columns, levels, values, variances = by_longitude(
        obs_column, [obs_column, obs_level, obs_value, obs_variance]
    )

    flat_column = columns.reshape(-1)
    flat_level = levels.reshape(-1)
    slab = (flat_level % own_levels) * parts + flat_column // part_columns
    owned = flat_level // own_levels == c
    picked = jnp.take(prior, flat_column % part_columns, axis=2)
    mine = (slab[None, :] == jnp.arange(SLABS, dtype=jnp.int32)[:, None]) & owned[None, :]
    picked = jnp.sum(jnp.where(mine[None], picked, 0.0), axis=1)
    picked = jnp.pad(picked, ((0, -own_members % 8), (0, 0)))

    prior = prior.reshape(own_members, SLABS, tiles, LANES).transpose(2, 0, 1, 3)
    prior = prior.reshape(tiles, own_members * SLABS, LANES)
    tile, obs = exchange_in(prior, picked, mem_n, col_n)
    obs = obs[:, :own_members].reshape(members, NB, P_SIZE)

    rows = (columns // NLON).astype(jnp.float32)
    lons = (columns % NLON).astype(jnp.float32)
    scale = 1.0 / (members - 1)
    state = [obs[:, b] for b in range(NB)]
    anoms, weights = [], []
    for b in range(NB):
        obs_anom, weight = obs_weights(state[b], values[b], variances[b])
        anoms.append(obs_anom * scale)
        weights.append(weight)
        for later in range(b + 1, NB):
            anomalies = state[later] - jnp.mean(state[later], axis=0)[None]
            cov = jnp.einsum(
                "kp,kc->pc",
                obs_anom * scale,
                anomalies,
                precision=lax.Precision.HIGHEST,
                preferred_element_type=jnp.float32,
            )
            gain = cov * taper_of(
                rows[later][None, :], lons[later][None, :], rows[b][:, None], lons[b][:, None]
            )
            state[later] = state[later] + jnp.einsum(
                "kp,pc->kc",
                weight,
                gain,
                precision=lax.Precision.HIGHEST,
                preferred_element_type=jnp.float32,
            )

    extra = PADDED - P_SIZE
    high, low = split_outside(jnp.stack(anoms).transpose(0, 2, 1))
    anom = jnp.pad(jnp.concatenate([high, high, low], axis=2), ((0, 0), (0, extra), (0, 0)))
    weight = jnp.pad(jnp.stack(weights), ((0, 0), (0, 0), (0, extra)))
    weight = weight.reshape(NB, members, CHUNKS, CHUNK).transpose(0, 2, 1, 3)
    high, low = split_outside(weight)
    weight = jnp.concatenate([high, high, low], axis=3)
    obs_row = jnp.pad(rows, ((0, 0), (0, extra)))[:, :, None]
    obs_lon = jnp.pad(lons, ((0, 0), (0, extra)))[:, :, None]

    slabs = jnp.arange(SLABS, dtype=jnp.int32)
    first_row = ((slabs % parts) * part_columns + m * width) // NLON
    done = update(
        tile, near_blocks(columns), first_row, anom, weight, obs_row, obs_lon, parts == 1
    )
    out = exchange_out(done, mem_n).reshape(tiles, own_members, SLABS, LANES)
    out = out.transpose(1, 2, 0, 3)
    return out.reshape(own_members, own_levels, all_columns)


def solution(mesh):
    return jax.shard_map(
        local,
        mesh=mesh,
        in_specs=(P("mem", "col", None), P(), P(), P(), P()),
        out_specs=P("mem", "col", None),
        check_vma=False,
    )
```

```python
import functools

import jax
import jax.numpy as jnp
from jax import lax
from jax.experimental import pallas as pl
from jax.experimental.pallas import tpu as pltpu
from jax.sharding import PartitionSpec as P

NLON = 768
P_SIZE = 512
NB = 2
LOCR = 6
REACH = 2 * LOCR
LANES = 128
BLOCKS = NLON // LANES
CHUNK = 80
CHUNKS = -(-P_SIZE // CHUNK)
PADDED = CHUNK * CHUNKS
SLABS = 4
GROUP = 4
HALVES = 2
MESH = pl.DeviceIdType.MESH


def gc_taper(squared_gap):
    scaled = jnp.sqrt(squared_gap) * (1.0 / LOCR)
    near_part = (
        ((-0.25 * scaled + 0.5) * scaled + 0.625) * scaled - 5.0 / 3.0
    ) * scaled * scaled + 1.0
    bounded = jnp.maximum(scaled, 1.0)
    far_part = (
        ((((scaled / 12.0 - 0.5) * scaled + 0.625) * scaled + 5.0 / 3.0) * scaled - 5.0) * scaled
        + 4.0
        - 2.0 / (3.0 * bounded)
    )
    return jnp.where(
        squared_gap < LOCR * LOCR,
        near_part,
        jnp.where(squared_gap < 4 * LOCR * LOCR, far_part, 0.0),
    )


def taper_of(rows, lons, obs_rows, obs_lons):
    row_gap = rows - obs_rows
    lon_gap = jnp.abs(lons - obs_lons)
    lon_gap = jnp.minimum(lon_gap, NLON - lon_gap)
    return gc_taper(row_gap * row_gap + lon_gap * lon_gap)


def obs_weights(picked, values, variances):
    members = picked.shape[0]
    obs_mean = jnp.mean(picked, axis=0)
    obs_anom = picked - obs_mean[None, :]
    obs_total = jnp.sum(obs_anom * obs_anom, axis=0) / (members - 1) + variances
    mean_gain = (values - obs_mean) / obs_total
    root_gain = 1.0 / (obs_total * (1.0 + jnp.sqrt(variances / obs_total)))
    weights = mean_gain[None, :] - root_gain[None, :] * obs_anom
    return (obs_anom, weights)


def split(x):
    high = x.astype(jnp.bfloat16)
    low = (x - high.astype(jnp.float32)).astype(jnp.bfloat16)
    return high, low


def split_outside(x):
    high = lax.reduce_precision(x, exponent_bits=8, mantissa_bits=7)
    return high.astype(jnp.bfloat16), (x - high).astype(jnp.bfloat16)


def pick_kernel(own_members, row, lane, owned, prior, out):
    stride = prior.shape[0] // own_members
    lanes = lax.broadcasted_iota(jnp.int32, (1, LANES), 1)

    def block(i, carry):
        def one(j, total):
            at = i * LANES + j
            values = prior[pl.ds(row[at], own_members, stride=stride), :]
            turned = pltpu.roll(values, lax.rem(j - lane[at] + LANES, LANES), 1)
            return jnp.where(lanes == jnp.where(owned[at] != 0, j, -1), turned, total)

        total = lax.fori_loop(0, LANES, one, jnp.zeros((own_members, LANES), jnp.float32), unroll=8)
        out[i, :own_members, :] = total
        return carry

    out[...] = jnp.zeros_like(out)
    lax.fori_loop(0, out.shape[0], block, 0)


def pick(prior, row, lane, owned, own_members):
    scalars = pl.BlockSpec(memory_space=pltpu.SMEM)
    blocks = row.shape[0] // LANES
    return pl.pallas_call(
        functools.partial(pick_kernel, own_members),
        out_shape=jax.ShapeDtypeStruct(
            (blocks, own_members + -own_members % 8, LANES), jnp.float32
        ),
        in_specs=[scalars, scalars, scalars, pl.BlockSpec(memory_space=pltpu.VMEM)],
        out_specs=pl.BlockSpec(memory_space=pltpu.VMEM),
        compiler_params=pltpu.CompilerParams(vmem_limit_bytes=16 * 1024 * 1024),
        cost_estimate=pl.CostEstimate(flops=10**10, bytes_accessed=10**7, transcendentals=0),
        name="pick",
    )(row, lane, owned, prior)


def gather_kernel(mem_n, col_n, picked, obs, slots, total, psend, precv, osend, orecv):
    m = lax.axis_index("mem")
    c = lax.axis_index("col")
    barrier = pltpu.get_barrier_semaphore()
    for j in range(1, mem_n):
        pl.semaphore_signal(barrier, inc=1, device_id=(lax.rem(m + j, mem_n), c), device_id_type=MESH)
    for j in range(1, col_n):
        pl.semaphore_signal(barrier, inc=1, device_id=(m, lax.rem(c + j, col_n)), device_id_type=MESH)
    pl.semaphore_wait(barrier, mem_n + col_n - 2)

    picks = []
    for j in range(1, col_n):
        copy = pltpu.make_async_remote_copy(
            src_ref=picked,
            dst_ref=slots.at[j],
            send_sem=psend.at[j],
            recv_sem=precv.at[j],
            device_id=(m, lax.rem(c + j, col_n)),
            device_id_type=MESH,
        )
        copy.start()
        picks.append(copy)
    for copy in picks:
        copy.wait_recv()
    summed = picked[...]
    for j in range(1, col_n):
        summed = summed + slots[j]
    total[...] = summed
    obs[m] = summed
    shares = []
    for j in range(1, mem_n):
        copy = pltpu.make_async_remote_copy(
            src_ref=total,
            dst_ref=obs.at[m],
            send_sem=osend.at[j],
            recv_sem=orecv.at[j],
            device_id=(lax.rem(m + j, mem_n), c),
            device_id_type=MESH,
        )
        copy.start()
        shares.append(copy)
    for copy in shares:
        copy.wait()
    for copy in picks:
        copy.wait_send()


def gather(picked, mem_n, col_n):
    return pl.pallas_call(
        functools.partial(gather_kernel, mem_n, col_n),
        out_shape=jax.ShapeDtypeStruct((mem_n,) + picked.shape, jnp.float32),
        in_specs=[pl.BlockSpec(memory_space=pltpu.VMEM)],
        out_specs=pl.BlockSpec(memory_space=pltpu.VMEM),
        scratch_shapes=[
            pltpu.VMEM((col_n,) + picked.shape, jnp.float32),
            pltpu.VMEM(picked.shape, jnp.float32),
            pltpu.SemaphoreType.DMA((col_n,)),
            pltpu.SemaphoreType.DMA((col_n,)),
            pltpu.SemaphoreType.DMA((mem_n,)),
            pltpu.SemaphoreType.DMA((mem_n,)),
        ],
        compiler_params=pltpu.CompilerParams(collective_id=0, has_side_effects=True),
        cost_estimate=pl.CostEstimate(flops=2 * 10**10, bytes_accessed=10**6, transcendentals=0),
        name="gather",
    )(picked)


def join_kernel(mem_n, *refs):
    pieces, out, sems = refs[:-2], refs[-2], refs[-1]
    m = lax.axis_index("mem")
    rows = pieces[0].shape[1]
    copies = []
    for i, piece in enumerate(pieces):
        half, j = divmod(i, mem_n)
        at = (jnp.bitwise_xor(m, j) * HALVES + half) * rows
        copy = pltpu.make_async_copy(
            piece, out.at[:, pl.ds(pl.multiple_of(at, 8), rows)], sems.at[i]
        )
        copy.start()
        copies.append(copy)
    for copy in copies:
        copy.wait()


def join(pieces, mem_n):
    own_members, rows, lanes = pieces[0].shape
    return pl.pallas_call(
        functools.partial(join_kernel, mem_n),
        out_shape=jax.ShapeDtypeStruct((own_members, rows * len(pieces), lanes), jnp.float32),
        in_specs=[pl.BlockSpec(memory_space=pl.ANY)] * len(pieces),
        out_specs=pl.BlockSpec(memory_space=pl.ANY),
        scratch_shapes=[pltpu.SemaphoreType.DMA((len(pieces),))],
        name="join",
    )(*pieces)


def update_kernel(mem_n, members, shared, *refs):
    near, first_row, anom, weight, obs_row, obs_lon = refs[:6]
    pieces, results = refs[6 : 6 + mem_n], refs[6 + mem_n : 6 + 2 * mem_n]
    tile, current, spread, sems = refs[6 + 2 * mem_n :]
    piece_rows = pieces[0].shape[0]
    stride = tile.shape[0] // members
    groups = stride // (SLABS * BLOCKS * GROUP)
    span = GROUP * LANES
    copies = [
        pltpu.make_async_copy(piece, tile.at[pl.ds(j * piece_rows, piece_rows)], sems.at[j])
        for j, piece in enumerate(pieces)
    ]
    for copy in copies:
        copy.start()
    for copy in copies:
        copy.wait()
    lane = lax.broadcasted_iota(jnp.int32, (1, LANES), 1)

    def step(index, carry):
        block = index // groups
        group = lax.rem(index, groups)
        starts = [((group * GROUP + r) * BLOCKS + block) * SLABS for r in range(GROUP)]
        for s in range(SLABS):
            for r in range(GROUP):
                at = s * span + r * LANES
                current[:, at : at + LANES] = tile[
                    pl.ds(starts[r] + s, members, stride=stride), :
                ]
        lons = (block * LANES + lane).astype(jnp.float32)
        for b in range(NB):
            for s in range(SLABS):
                part = current[:, s * span : (s + 1) * span]
                high, low = split(part - jnp.mean(part, axis=0, keepdims=True))
                spread[:, s * span : (s + 1) * span] = jnp.concatenate([high, low, high], axis=0)
            for chunk in range(CHUNKS):

                @pl.when(near[b, chunk, block] != 0)
                def _():
                    here = pl.ds(chunk * CHUNK, CHUNK)
                    rows_here = obs_row[b, here, :]
                    lons_here = obs_lon[b, here, :]
                    gains = None
                    for s in range(SLABS):
                        if s == 0 or not shared:
                            gains = jnp.concatenate(
                                [
                                    taper_of(
                                        (first_row[s] + group * GROUP + r).astype(jnp.float32),
                                        lons,
                                        rows_here,
                                        lons_here,
                                    )
                                    for r in range(GROUP)
                                ],
                                axis=1,
                            )
                        cov = jnp.dot(
                            anom[b, here, :],
                            spread[:, s * span : (s + 1) * span],
                            preferred_element_type=jnp.float32,
                        )
                        high, low = split(cov * gains)
                        current[:, s * span : (s + 1) * span] += jnp.dot(
                            weight[b, chunk],
                            jnp.concatenate([high, low, high], axis=0),
                            preferred_element_type=jnp.float32,
                        )
        for s in range(SLABS):
            for r in range(GROUP):
                at = s * span + r * LANES
                tile[pl.ds(starts[r] + s, members, stride=stride), :] = current[
                    :, at : at + LANES
                ]
        return carry

    lax.fori_loop(0, BLOCKS * groups, step, 0)
    copies = [
        pltpu.make_async_copy(tile.at[pl.ds(j * piece_rows, piece_rows)], result, sems.at[j])
        for j, result in enumerate(results)
    ]
    for copy in copies:
        copy.start()
    for copy in copies:
        copy.wait()


def update(pieces, near, first_row, anom, weight, obs_row, obs_lon, members, shared):
    mem_n = len(pieces)
    piece_rows = pieces[0].shape[0]
    whole = pl.BlockSpec(memory_space=pltpu.VMEM)
    scalars = pl.BlockSpec(memory_space=pltpu.SMEM)
    hbm = pl.BlockSpec(memory_space=pl.ANY)
    return pl.pallas_call(
        functools.partial(update_kernel, mem_n, members, shared),
        out_shape=[jax.ShapeDtypeStruct(p.shape, jnp.float32) for p in pieces],
        in_specs=[scalars, scalars, whole, whole, whole, whole] + [hbm] * mem_n,
        out_specs=[hbm] * mem_n,
        scratch_shapes=[
            pltpu.VMEM((mem_n * piece_rows, LANES), jnp.float32),
            pltpu.VMEM((members, SLABS * GROUP * LANES), jnp.float32),
            pltpu.VMEM((3 * members, SLABS * GROUP * LANES), jnp.bfloat16),
            pltpu.SemaphoreType.DMA((mem_n,)),
        ],
        compiler_params=pltpu.CompilerParams(vmem_limit_bytes=24 * 1024 * 1024),
        cost_estimate=pl.CostEstimate(flops=4 * 10**10, bytes_accessed=10**7, transcendentals=0),
        name="update",
    )(near, first_row, anom, weight, obs_row, obs_lon, *pieces)


def by_longitude(columns, arrays):
    lons = columns % NLON
    count = columns.shape[1]
    index = jnp.arange(count, dtype=jnp.int32)
    before = (lons[:, :, None] < lons[:, None, :]) | (
        (lons[:, :, None] == lons[:, None, :]) & (index[:, None] < index[None, :])[None]
    )
    rank = jnp.sum(before.astype(jnp.int32), axis=1)
    chosen = rank[:, :, None] == index[None, None, :]
    return [jnp.sum(jnp.where(chosen, a[:, :, None], jnp.zeros((), a.dtype)), axis=1) for a in arrays]


def near_blocks(columns):
    lons = columns % NLON
    past = (lons[:, :, None] - (jnp.arange(BLOCKS, dtype=jnp.int32) * LANES)[None, None, :]) % NLON
    hit = (past < LANES + REACH) | (past > NLON - REACH)
    hit = jnp.pad(hit, ((0, 0), (0, PADDED - P_SIZE), (0, 0)))
    return jnp.any(hit.reshape(NB, CHUNKS, CHUNK, BLOCKS), axis=2).astype(jnp.int32)


def local(prior, obs_column, obs_level, obs_value, obs_variance):
    own_members, own_levels, all_columns = prior.shape
    mem_n = lax.axis_size("mem")
    col_n = lax.axis_size("col")
    m = lax.axis_index("mem")
    c = lax.axis_index("col")
    members = own_members * mem_n
    parts = SLABS // own_levels
    part_columns = all_columns // parts
    width = part_columns // mem_n
    tiles = part_columns // LANES
    tiles = part_columns // LANES
    prior = prior.reshape(own_members, SLABS, tiles, LANES).transpose(0, 2, 1, 3)
    prior = prior.reshape(own_members, tiles * SLABS, LANES)
    piece = tiles * SLABS // (mem_n * HALVES)
    peers = [jnp.bitwise_xor(m, j) for j in range(mem_n)]
    pairs = [[(i, i ^ j) for i in range(mem_n)] for j in range(mem_n)]

    def swap(parts):
        return [parts[0]] + [lax.ppermute(parts[j], "mem", pairs[j]) for j in range(1, mem_n)]

    arrived = []
    for half in range(HALVES):
        sent = [
            lax.dynamic_slice_in_dim(prior, (peer * HALVES + half) * piece, piece, 1)
            for peer in peers
        ]
        arrived.append(swap(sent))

    columns, levels, values, variances = by_longitude(
        obs_column, [obs_column, obs_level, obs_value, obs_variance]
    )

    flat_column = columns.reshape(-1)
    flat_level = levels.reshape(-1)
    slab = (flat_level % own_levels) * parts + flat_column // part_columns
    part_column = flat_column % part_columns
    owned = flat_level // own_levels == c
    row = part_column // LANES * SLABS + slab
    picked = pick(
        prior.reshape(own_members * tiles * SLABS, LANES),
        jnp.where(owned, row, 0),
        part_column % LANES,
        owned.astype(jnp.int32),
        own_members,
    )
    obs = gather(picked, mem_n, col_n)[:, :, :own_members]
    obs = jnp.take(obs, jnp.stack(peers), axis=0).transpose(0, 2, 1, 3)
    obs = obs.reshape(members, NB, P_SIZE)

    rows = (columns // NLON).astype(jnp.float32)
    lons = (columns % NLON).astype(jnp.float32)
    scale = 1.0 / (members - 1)
    state = [obs[:, b] for b in range(NB)]
    anoms, weights = [], []
    for b in range(NB):
        obs_anom, weight = obs_weights(state[b], values[b], variances[b])
        anoms.append(obs_anom * scale)
        weights.append(weight)
        for later in range(b + 1, NB):
            anomalies = state[later] - jnp.mean(state[later], axis=0)[None]
            cov = jnp.einsum(
                "kp,kc->pc",
                obs_anom * scale,
                anomalies,
                precision=lax.Precision.HIGHEST,
                preferred_element_type=jnp.float32,
            )
            gain = cov * taper_of(
                rows[later][None, :], lons[later][None, :], rows[b][:, None], lons[b][:, None]
            )
            state[later] = state[later] + jnp.einsum(
                "kp,pc->kc",
                weight,
                gain,
                precision=lax.Precision.HIGHEST,
                preferred_element_type=jnp.float32,
            )

    extra = PADDED - P_SIZE
    high, low = split_outside(jnp.stack(anoms).transpose(0, 2, 1))
    anom = jnp.pad(jnp.concatenate([high, high, low], axis=2), ((0, 0), (0, extra), (0, 0)))
    weight = jnp.pad(jnp.stack(weights), ((0, 0), (0, 0), (0, extra)))
    weight = weight.reshape(NB, members, CHUNKS, CHUNK).transpose(0, 2, 1, 3)
    high, low = split_outside(weight)
    weight = jnp.concatenate([high, high, low], axis=3)
    obs_row = jnp.pad(rows, ((0, 0), (0, extra)))[:, :, None]
    obs_lon = jnp.pad(lons, ((0, 0), (0, extra)))[:, :, None]

    slabs = jnp.arange(SLABS, dtype=jnp.int32)
    near = near_blocks(columns)
    pieces = []
    for half in range(HALVES):
        first_row = (slabs % parts) * part_columns + m * width + half * (width // HALVES)
        done = update(
            [p.reshape(own_members * piece, LANES) for p in arrived[half]],
            near,
            first_row // NLON,
            anom,
            weight,
            obs_row,
            obs_lon,
            members,
            parts == 1,
        )
        pieces += [p.reshape(own_members, piece, LANES) for p in swap(done)]
    out = join(pieces, mem_n).reshape(own_members, tiles, SLABS, LANES)
    out = out.transpose(0, 2, 1, 3)
    return out.reshape(own_members, own_levels, all_columns)


def solution(mesh):
    return jax.shard_map(
        local,
        mesh=mesh,
        in_specs=(P("mem", "col", None), P(), P(), P(), P()),
        out_specs=P("mem", "col", None),
        check_vma=False,
    )
```

```python
import functools

import jax
import jax.numpy as jnp
from jax import lax
from jax.experimental import pallas as pl
from jax.experimental.pallas import tpu as pltpu
from jax.sharding import PartitionSpec as P

NLON = 768
P_SIZE = 512
NB = 2
LOCR = 6
REACH = 2 * LOCR
LANES = 128
BLOCKS = NLON // LANES
CHUNK = 80
CHUNKS = -(-P_SIZE // CHUNK)
PADDED = CHUNK * CHUNKS
SLABS = 4
GROUP = 4
HALVES = 2
MESH = pl.DeviceIdType.MESH


def gc_taper(squared_gap):
    scaled = jnp.sqrt(squared_gap) * (1.0 / LOCR)
    near_part = (
        ((-0.25 * scaled + 0.5) * scaled + 0.625) * scaled - 5.0 / 3.0
    ) * scaled * scaled + 1.0
    bounded = jnp.maximum(scaled, 1.0)
    far_part = (
        ((((scaled / 12.0 - 0.5) * scaled + 0.625) * scaled + 5.0 / 3.0) * scaled - 5.0) * scaled
        + 4.0
        - 2.0 / (3.0 * bounded)
    )
    return jnp.where(
        squared_gap < LOCR * LOCR,
        near_part,
        jnp.where(squared_gap < 4 * LOCR * LOCR, far_part, 0.0),
    )


def taper_of(rows, lons, obs_rows, obs_lons):
    row_gap = rows - obs_rows
    lon_gap = jnp.abs(lons - obs_lons)
    lon_gap = jnp.minimum(lon_gap, NLON - lon_gap)
    return gc_taper(row_gap * row_gap + lon_gap * lon_gap)


def obs_weights(picked, values, variances):
    members = picked.shape[0]
    obs_mean = jnp.mean(picked, axis=0)
    obs_anom = picked - obs_mean[None, :]
    obs_total = jnp.sum(obs_anom * obs_anom, axis=0) / (members - 1) + variances
    mean_gain = (values - obs_mean) / obs_total
    root_gain = 1.0 / (obs_total * (1.0 + jnp.sqrt(variances / obs_total)))
    weights = mean_gain[None, :] - root_gain[None, :] * obs_anom
    return (obs_anom, weights)


def split(x):
    high = x.astype(jnp.bfloat16)
    low = (x - high.astype(jnp.float32)).astype(jnp.bfloat16)
    return high, low


def split_outside(x):
    high = lax.reduce_precision(x, exponent_bits=8, mantissa_bits=7)
    return high.astype(jnp.bfloat16), (x - high).astype(jnp.bfloat16)


def pick_kernel(own_members, row, lane, owned, prior, out):
    stride = prior.shape[0] // own_members
    lanes = lax.broadcasted_iota(jnp.int32, (1, LANES), 1)

    def block(i, carry):
        def one(j, total):
            at = i * LANES + j
            values = prior[pl.ds(row[at], own_members, stride=stride), :]
            turned = pltpu.roll(values, lax.rem(j - lane[at] + LANES, LANES), 1)
            return jnp.where(lanes == jnp.where(owned[at] != 0, j, -1), turned, total)

        total = lax.fori_loop(0, LANES, one, jnp.zeros((own_members, LANES), jnp.float32), unroll=8)
        out[i, :own_members, :] = total
        return carry

    out[...] = jnp.zeros_like(out)
    lax.fori_loop(0, out.shape[0], block, 0)


def pick(prior, row, lane, owned, own_members):
    scalars = pl.BlockSpec(memory_space=pltpu.SMEM)
    blocks = row.shape[0] // LANES
    return pl.pallas_call(
        functools.partial(pick_kernel, own_members),
        out_shape=jax.ShapeDtypeStruct(
            (blocks, own_members + -own_members % 8, LANES), jnp.float32
        ),
        in_specs=[scalars, scalars, scalars, pl.BlockSpec(memory_space=pltpu.VMEM)],
        out_specs=pl.BlockSpec(memory_space=pltpu.VMEM),
        compiler_params=pltpu.CompilerParams(vmem_limit_bytes=16 * 1024 * 1024),
        cost_estimate=pl.CostEstimate(flops=10**10, bytes_accessed=10**7, transcendentals=0),
        name="pick",
    )(row, lane, owned, prior)


def gather_kernel(mem_n, col_n, picked, obs, slots, total, psend, precv, osend, orecv):
    m = lax.axis_index("mem")
    c = lax.axis_index("col")
    barrier = pltpu.get_barrier_semaphore()
    for j in range(1, mem_n):
        pl.semaphore_signal(barrier, inc=1, device_id=(lax.rem(m + j, mem_n), c), device_id_type=MESH)
    for j in range(1, col_n):
        pl.semaphore_signal(barrier, inc=1, device_id=(m, lax.rem(c + j, col_n)), device_id_type=MESH)
    pl.semaphore_wait(barrier, mem_n + col_n - 2)

    picks = []
    for j in range(1, col_n):
        copy = pltpu.make_async_remote_copy(
            src_ref=picked,
            dst_ref=slots.at[j],
            send_sem=psend.at[j],
            recv_sem=precv.at[j],
            device_id=(m, lax.rem(c + j, col_n)),
            device_id_type=MESH,
        )
        copy.start()
        picks.append(copy)
    for copy in picks:
        copy.wait_recv()
    summed = picked[...]
    for j in range(1, col_n):
        summed = summed + slots[j]
    total[...] = summed
    obs[m] = summed
    shares = []
    for j in range(1, mem_n):
        copy = pltpu.make_async_remote_copy(
            src_ref=total,
            dst_ref=obs.at[m],
            send_sem=osend.at[j],
            recv_sem=orecv.at[j],
            device_id=(lax.rem(m + j, mem_n), c),
            device_id_type=MESH,
        )
        copy.start()
        shares.append(copy)
    for copy in shares:
        copy.wait()
    for copy in picks:
        copy.wait_send()


def gather(picked, mem_n, col_n):
    return pl.pallas_call(
        functools.partial(gather_kernel, mem_n, col_n),
        out_shape=jax.ShapeDtypeStruct((mem_n,) + picked.shape, jnp.float32),
        in_specs=[pl.BlockSpec(memory_space=pltpu.VMEM)],
        out_specs=pl.BlockSpec(memory_space=pltpu.VMEM),
        scratch_shapes=[
            pltpu.VMEM((col_n,) + picked.shape, jnp.float32),
            pltpu.VMEM(picked.shape, jnp.float32),
            pltpu.SemaphoreType.DMA((col_n,)),
            pltpu.SemaphoreType.DMA((col_n,)),
            pltpu.SemaphoreType.DMA((mem_n,)),
            pltpu.SemaphoreType.DMA((mem_n,)),
        ],
        compiler_params=pltpu.CompilerParams(collective_id=0, has_side_effects=True),
        cost_estimate=pl.CostEstimate(flops=2 * 10**10, bytes_accessed=10**6, transcendentals=0),
        name="gather",
    )(picked)


def join_kernel(mem_n, *refs):
    pieces, out, sems = refs[:-2], refs[-2], refs[-1]
    m = lax.axis_index("mem")
    rows = pieces[0].shape[1]
    copies = []
    for i, piece in enumerate(pieces):
        half, j = divmod(i, mem_n)
        at = (jnp.bitwise_xor(m, j) * HALVES + half) * rows
        copy = pltpu.make_async_copy(
            piece, out.at[:, pl.ds(pl.multiple_of(at, 8), rows)], sems.at[i]
        )
        copy.start()
        copies.append(copy)
    for copy in copies:
        copy.wait()


def join(pieces, mem_n):
    own_members, rows, lanes = pieces[0].shape
    return pl.pallas_call(
        functools.partial(join_kernel, mem_n),
        out_shape=jax.ShapeDtypeStruct((own_members, rows * len(pieces), lanes), jnp.float32),
        in_specs=[pl.BlockSpec(memory_space=pltpu.VMEM)] * len(pieces),
        out_specs=pl.BlockSpec(memory_space=pl.ANY),
        scratch_shapes=[pltpu.SemaphoreType.DMA((len(pieces),))],
        compiler_params=pltpu.CompilerParams(vmem_limit_bytes=16 * 1024 * 1024),
        name="join",
    )(*pieces)


def update_kernel(mem_n, members, shared, *refs):
    near, first_row, anom, weight, obs_row, obs_lon = refs[:6]
    pieces, results = refs[6 : 6 + mem_n], refs[6 + mem_n : 6 + 2 * mem_n]
    tile, current, spread, sems = refs[6 + 2 * mem_n :]
    piece_rows = pieces[0].shape[0]
    stride = tile.shape[0] // members
    groups = stride // (SLABS * BLOCKS * GROUP)
    span = GROUP * LANES
    copies = [
        pltpu.make_async_copy(piece, tile.at[pl.ds(j * piece_rows, piece_rows)], sems.at[j])
        for j, piece in enumerate(pieces)
    ]
    for copy in copies:
        copy.start()
    for copy in copies:
        copy.wait()
    lane = lax.broadcasted_iota(jnp.int32, (1, LANES), 1)

    def step(index, carry):
        block = index // groups
        group = lax.rem(index, groups)
        starts = [((group * GROUP + r) * BLOCKS + block) * SLABS for r in range(GROUP)]
        for s in range(SLABS):
            for r in range(GROUP):
                at = s * span + r * LANES
                current[:, at : at + LANES] = tile[
                    pl.ds(starts[r] + s, members, stride=stride), :
                ]
        lons = (block * LANES + lane).astype(jnp.float32)
        for b in range(NB):
            for s in range(SLABS):
                part = current[:, s * span : (s + 1) * span]
                high, low = split(part - jnp.mean(part, axis=0, keepdims=True))
                spread[:, s * span : (s + 1) * span] = jnp.concatenate([high, low, high], axis=0)
            for chunk in range(CHUNKS):

                @pl.when(near[b, chunk, block] != 0)
                def _():
                    here = pl.ds(chunk * CHUNK, CHUNK)
                    rows_here = obs_row[b, here, :]
                    lons_here = obs_lon[b, here, :]
                    gains = None
                    for s in range(SLABS):
                        if s == 0 or not shared:
                            gains = jnp.concatenate(
                                [
                                    taper_of(
                                        (first_row[s] + group * GROUP + r).astype(jnp.float32),
                                        lons,
                                        rows_here,
                                        lons_here,
                                    )
                                    for r in range(GROUP)
                                ],
                                axis=1,
                            )
                        cov = jnp.dot(
                            anom[b, here, :],
                            spread[:, s * span : (s + 1) * span],
                            preferred_element_type=jnp.float32,
                        )
                        high, low = split(cov * gains)
                        current[:, s * span : (s + 1) * span] += jnp.dot(
                            weight[b, chunk],
                            jnp.concatenate([high, low, high], axis=0),
                            preferred_element_type=jnp.float32,
                        )
        for s in range(SLABS):
            for r in range(GROUP):
                at = s * span + r * LANES
                tile[pl.ds(starts[r] + s, members, stride=stride), :] = current[
                    :, at : at + LANES
                ]
        return carry

    lax.fori_loop(0, BLOCKS * groups, step, 0)
    copies = [
        pltpu.make_async_copy(tile.at[pl.ds(j * piece_rows, piece_rows)], result, sems.at[j])
        for j, result in enumerate(results)
    ]
    for copy in copies:
        copy.start()
    for copy in copies:
        copy.wait()


def update(pieces, near, first_row, anom, weight, obs_row, obs_lon, members, shared):
    mem_n = len(pieces)
    piece_rows = pieces[0].shape[0]
    whole = pl.BlockSpec(memory_space=pltpu.VMEM)
    scalars = pl.BlockSpec(memory_space=pltpu.SMEM)
    hbm = pl.BlockSpec(memory_space=pl.ANY)
    return pl.pallas_call(
        functools.partial(update_kernel, mem_n, members, shared),
        out_shape=[jax.ShapeDtypeStruct(p.shape, jnp.float32) for p in pieces],
        in_specs=[scalars, scalars, whole, whole, whole, whole] + [hbm] * mem_n,
        out_specs=[hbm] * mem_n,
        scratch_shapes=[
            pltpu.VMEM((mem_n * piece_rows, LANES), jnp.float32),
            pltpu.VMEM((members, SLABS * GROUP * LANES), jnp.float32),
            pltpu.VMEM((3 * members, SLABS * GROUP * LANES), jnp.bfloat16),
            pltpu.SemaphoreType.DMA((mem_n,)),
        ],
        compiler_params=pltpu.CompilerParams(vmem_limit_bytes=24 * 1024 * 1024),
        cost_estimate=pl.CostEstimate(flops=4 * 10**10, bytes_accessed=10**7, transcendentals=0),
        name="update",
    )(near, first_row, anom, weight, obs_row, obs_lon, *pieces)


def by_longitude(columns, arrays):
    lons = columns % NLON
    count = columns.shape[1]
    index = jnp.arange(count, dtype=jnp.int32)
    before = (lons[:, :, None] < lons[:, None, :]) | (
        (lons[:, :, None] == lons[:, None, :]) & (index[:, None] < index[None, :])[None]
    )
    rank = jnp.sum(before.astype(jnp.int32), axis=1)
    chosen = rank[:, :, None] == index[None, None, :]
    return [jnp.sum(jnp.where(chosen, a[:, :, None], jnp.zeros((), a.dtype)), axis=1) for a in arrays]


def near_blocks(columns):
    lons = columns % NLON
    past = (lons[:, :, None] - (jnp.arange(BLOCKS, dtype=jnp.int32) * LANES)[None, None, :]) % NLON
    hit = (past < LANES + REACH) | (past > NLON - REACH)
    hit = jnp.pad(hit, ((0, 0), (0, PADDED - P_SIZE), (0, 0)))
    return jnp.any(hit.reshape(NB, CHUNKS, CHUNK, BLOCKS), axis=2).astype(jnp.int32)


def local(prior, obs_column, obs_level, obs_value, obs_variance):
    own_members, own_levels, all_columns = prior.shape
    mem_n = lax.axis_size("mem")
    col_n = lax.axis_size("col")
    m = lax.axis_index("mem")
    c = lax.axis_index("col")
    members = own_members * mem_n
    parts = SLABS // own_levels
    part_columns = all_columns // parts
    width = part_columns // mem_n
    tiles = part_columns // LANES
    tiles = part_columns // LANES
    prior = prior.reshape(own_members, SLABS, tiles, LANES).transpose(0, 2, 1, 3)
    prior = prior.reshape(own_members, tiles * SLABS, LANES)
    piece = tiles * SLABS // (mem_n * HALVES)
    peers = [jnp.bitwise_xor(m, j) for j in range(mem_n)]
    pairs = [[(i, i ^ j) for i in range(mem_n)] for j in range(mem_n)]

    def swap(parts):
        return [parts[0]] + [lax.ppermute(parts[j], "mem", pairs[j]) for j in range(1, mem_n)]

    def fetch(half):
        return swap(
            [
                lax.dynamic_slice_in_dim(prior, (peer * HALVES + half) * piece, piece, 1)
                for peer in peers
            ]
        )

    arrived = [fetch(0)]

    columns, levels, values, variances = by_longitude(
        obs_column, [obs_column, obs_level, obs_value, obs_variance]
    )

    flat_column = columns.reshape(-1)
    flat_level = levels.reshape(-1)
    slab = (flat_level % own_levels) * parts + flat_column // part_columns
    part_column = flat_column % part_columns
    owned = flat_level // own_levels == c
    row = part_column // LANES * SLABS + slab
    picked = pick(
        prior.reshape(own_members * tiles * SLABS, LANES),
        jnp.where(owned, row, 0),
        part_column % LANES,
        owned.astype(jnp.int32),
        own_members,
    )
    obs = gather(picked, mem_n, col_n)
    for half in range(1, HALVES):
        prior, arrived[half - 1] = lax.optimization_barrier((prior, arrived[half - 1]))
        arrived.append(fetch(half))
    obs = obs[:, :, :own_members]
    obs = jnp.take(obs, jnp.stack(peers), axis=0).transpose(0, 2, 1, 3)
    obs = obs.reshape(members, NB, P_SIZE)

    rows = (columns // NLON).astype(jnp.float32)
    lons = (columns % NLON).astype(jnp.float32)
    scale = 1.0 / (members - 1)
    state = [obs[:, b] for b in range(NB)]
    anoms, weights = [], []
    for b in range(NB):
        obs_anom, weight = obs_weights(state[b], values[b], variances[b])
        anoms.append(obs_anom * scale)
        weights.append(weight)
        for later in range(b + 1, NB):
            anomalies = state[later] - jnp.mean(state[later], axis=0)[None]
            cov = jnp.einsum(
                "kp,kc->pc",
                obs_anom * scale,
                anomalies,
                precision=lax.Precision.HIGHEST,
                preferred_element_type=jnp.float32,
            )
            gain = cov * taper_of(
                rows[later][None, :], lons[later][None, :], rows[b][:, None], lons[b][:, None]
            )
            state[later] = state[later] + jnp.einsum(
                "kp,pc->kc",
                weight,
                gain,
                precision=lax.Precision.HIGHEST,
                preferred_element_type=jnp.float32,
            )

    extra = PADDED - P_SIZE
    high, low = split_outside(jnp.stack(anoms).transpose(0, 2, 1))
    anom = jnp.pad(jnp.concatenate([high, high, low], axis=2), ((0, 0), (0, extra), (0, 0)))
    weight = jnp.pad(jnp.stack(weights), ((0, 0), (0, 0), (0, extra)))
    weight = weight.reshape(NB, members, CHUNKS, CHUNK).transpose(0, 2, 1, 3)
    high, low = split_outside(weight)
    weight = jnp.concatenate([high, high, low], axis=3)
    obs_row = jnp.pad(rows, ((0, 0), (0, extra)))[:, :, None]
    obs_lon = jnp.pad(lons, ((0, 0), (0, extra)))[:, :, None]

    slabs = jnp.arange(SLABS, dtype=jnp.int32)
    near = near_blocks(columns)
    pieces = []
    for half in range(HALVES):
        first_row = (slabs % parts) * part_columns + m * width + half * (width // HALVES)
        done = update(
            [p.reshape(own_members * piece, LANES) for p in arrived[half]],
            near,
            first_row // NLON,
            anom,
            weight,
            obs_row,
            obs_lon,
            members,
            parts == 1,
        )
        pieces += [p.reshape(own_members, piece, LANES) for p in swap(done)]
    out = join(pieces, mem_n).reshape(own_members, tiles, SLABS, LANES)
    out = out.transpose(0, 2, 1, 3)
    return out.reshape(own_members, own_levels, all_columns)


def solution(mesh):
    return jax.shard_map(
        local,
        mesh=mesh,
        in_specs=(P("mem", "col", None), P(), P(), P(), P()),
        out_specs=P("mem", "col", None),
        check_vma=False,
    )
```

```python
import functools

import jax
import jax.numpy as jnp
from jax import lax
from jax.experimental import pallas as pl
from jax.experimental.pallas import tpu as pltpu
from jax.sharding import PartitionSpec as P

NLON = 768
P_SIZE = 512
NB = 2
LOCR = 6
REACH = 2 * LOCR
LANES = 128
BLOCKS = NLON // LANES
CHUNK = 80
CHUNKS = -(-P_SIZE // CHUNK)
PADDED = CHUNK * CHUNKS
SLABS = 4
GROUP = 2
HALVES = 4
MESH = pl.DeviceIdType.MESH


def gc_taper(squared_gap):
    scaled = jnp.sqrt(squared_gap) * (1.0 / LOCR)
    near_part = (
        ((-0.25 * scaled + 0.5) * scaled + 0.625) * scaled - 5.0 / 3.0
    ) * scaled * scaled + 1.0
    bounded = jnp.maximum(scaled, 1.0)
    far_part = (
        ((((scaled / 12.0 - 0.5) * scaled + 0.625) * scaled + 5.0 / 3.0) * scaled - 5.0) * scaled
        + 4.0
        - 2.0 / (3.0 * bounded)
    )
    return jnp.where(
        squared_gap < LOCR * LOCR,
        near_part,
        jnp.where(squared_gap < 4 * LOCR * LOCR, far_part, 0.0),
    )


def taper_of(rows, lons, obs_rows, obs_lons):
    row_gap = rows - obs_rows
    lon_gap = jnp.abs(lons - obs_lons)
    lon_gap = jnp.minimum(lon_gap, NLON - lon_gap)
    return gc_taper(row_gap * row_gap + lon_gap * lon_gap)


def obs_weights(picked, values, variances):
    members = picked.shape[0]
    obs_mean = jnp.mean(picked, axis=0)
    obs_anom = picked - obs_mean[None, :]
    obs_total = jnp.sum(obs_anom * obs_anom, axis=0) / (members - 1) + variances
    mean_gain = (values - obs_mean) / obs_total
    root_gain = 1.0 / (obs_total * (1.0 + jnp.sqrt(variances / obs_total)))
    weights = mean_gain[None, :] - root_gain[None, :] * obs_anom
    return (obs_anom, weights)


def split(x):
    high = x.astype(jnp.bfloat16)
    low = (x - high.astype(jnp.float32)).astype(jnp.bfloat16)
    return high, low


def split_outside(x):
    high = lax.reduce_precision(x, exponent_bits=8, mantissa_bits=7)
    return high.astype(jnp.bfloat16), (x - high).astype(jnp.bfloat16)


def pick_kernel(own_members, row, lane, owned, prior, out):
    stride = prior.shape[0] // own_members
    lanes = lax.broadcasted_iota(jnp.int32, (1, LANES), 1)

    def block(i, carry):
        def one(j, total):
            at = i * LANES + j
            values = prior[pl.ds(row[at], own_members, stride=stride), :]
            turned = pltpu.roll(values, lax.rem(j - lane[at] + LANES, LANES), 1)
            return jnp.where(lanes == jnp.where(owned[at] != 0, j, -1), turned, total)

        total = lax.fori_loop(0, LANES, one, jnp.zeros((own_members, LANES), jnp.float32), unroll=8)
        out[i, :own_members, :] = total
        return carry

    out[...] = jnp.zeros_like(out)
    lax.fori_loop(0, out.shape[0], block, 0)


def pick(prior, row, lane, owned, own_members):
    scalars = pl.BlockSpec(memory_space=pltpu.SMEM)
    blocks = row.shape[0] // LANES
    return pl.pallas_call(
        functools.partial(pick_kernel, own_members),
        out_shape=jax.ShapeDtypeStruct(
            (blocks, own_members + -own_members % 8, LANES), jnp.float32
        ),
        in_specs=[scalars, scalars, scalars, pl.BlockSpec(memory_space=pltpu.VMEM)],
        out_specs=pl.BlockSpec(memory_space=pltpu.VMEM),
        compiler_params=pltpu.CompilerParams(vmem_limit_bytes=16 * 1024 * 1024),
        cost_estimate=pl.CostEstimate(flops=10**10, bytes_accessed=10**7, transcendentals=0),
        name="pick",
    )(row, lane, owned, prior)


def gather_kernel(mem_n, col_n, picked, obs, slots, total, psend, precv, osend, orecv):
    m = lax.axis_index("mem")
    c = lax.axis_index("col")
    barrier = pltpu.get_barrier_semaphore()
    for j in range(1, mem_n):
        pl.semaphore_signal(barrier, inc=1, device_id=(lax.rem(m + j, mem_n), c), device_id_type=MESH)
    for j in range(1, col_n):
        pl.semaphore_signal(barrier, inc=1, device_id=(m, lax.rem(c + j, col_n)), device_id_type=MESH)
    pl.semaphore_wait(barrier, mem_n + col_n - 2)

    picks = []
    for j in range(1, col_n):
        copy = pltpu.make_async_remote_copy(
            src_ref=picked,
            dst_ref=slots.at[j],
            send_sem=psend.at[j],
            recv_sem=precv.at[j],
            device_id=(m, lax.rem(c + j, col_n)),
            device_id_type=MESH,
        )
        copy.start()
        picks.append(copy)
    for copy in picks:
        copy.wait_recv()
    summed = picked[...]
    for j in range(1, col_n):
        summed = summed + slots[j]
    total[...] = summed
    obs[m] = summed
    shares = []
    for j in range(1, mem_n):
        copy = pltpu.make_async_remote_copy(
            src_ref=total,
            dst_ref=obs.at[m],
            send_sem=osend.at[j],
            recv_sem=orecv.at[j],
            device_id=(lax.rem(m + j, mem_n), c),
            device_id_type=MESH,
        )
        copy.start()
        shares.append(copy)
    for copy in shares:
        copy.wait()
    for copy in picks:
        copy.wait_send()


def gather(picked, mem_n, col_n):
    return pl.pallas_call(
        functools.partial(gather_kernel, mem_n, col_n),
        out_shape=jax.ShapeDtypeStruct((mem_n,) + picked.shape, jnp.float32),
        in_specs=[pl.BlockSpec(memory_space=pltpu.VMEM)],
        out_specs=pl.BlockSpec(memory_space=pltpu.VMEM),
        scratch_shapes=[
            pltpu.VMEM((col_n,) + picked.shape, jnp.float32),
            pltpu.VMEM(picked.shape, jnp.float32),
            pltpu.SemaphoreType.DMA((col_n,)),
            pltpu.SemaphoreType.DMA((col_n,)),
            pltpu.SemaphoreType.DMA((mem_n,)),
            pltpu.SemaphoreType.DMA((mem_n,)),
        ],
        compiler_params=pltpu.CompilerParams(collective_id=0, has_side_effects=True),
        cost_estimate=pl.CostEstimate(flops=2 * 10**10, bytes_accessed=10**6, transcendentals=0),
        name="gather",
    )(picked)


def join_kernel(mem_n, *refs):
    pieces, out, sems = refs[:-2], refs[-2], refs[-1]
    m = lax.axis_index("mem")
    rows = pieces[0].shape[1]
    copies = []
    for i, piece in enumerate(pieces):
        half, j = divmod(i, mem_n)
        at = (jnp.bitwise_xor(m, j) * HALVES + half) * rows
        copy = pltpu.make_async_copy(
            piece, out.at[:, pl.ds(pl.multiple_of(at, 8), rows)], sems.at[i]
        )
        copy.start()
        copies.append(copy)
    for copy in copies:
        copy.wait()


def join(pieces, mem_n):
    own_members, rows, lanes = pieces[0].shape
    return pl.pallas_call(
        functools.partial(join_kernel, mem_n),
        out_shape=jax.ShapeDtypeStruct((own_members, rows * len(pieces), lanes), jnp.float32),
        in_specs=[pl.BlockSpec(memory_space=pltpu.VMEM)] * len(pieces),
        out_specs=pl.BlockSpec(memory_space=pl.ANY),
        scratch_shapes=[pltpu.SemaphoreType.DMA((len(pieces),))],
        compiler_params=pltpu.CompilerParams(vmem_limit_bytes=16 * 1024 * 1024),
        name="join",
    )(*pieces)


def update_kernel(mem_n, members, shared, *refs):
    near, first_row, anom, weight, obs_row, obs_lon = refs[:6]
    pieces, results = refs[6 : 6 + mem_n], refs[6 + mem_n : 6 + 2 * mem_n]
    tile, current, spread, sems = refs[6 + 2 * mem_n :]
    piece_rows = pieces[0].shape[0]
    stride = tile.shape[0] // members
    groups = stride // (SLABS * BLOCKS * GROUP)
    span = GROUP * LANES
    copies = [
        pltpu.make_async_copy(piece, tile.at[pl.ds(j * piece_rows, piece_rows)], sems.at[j])
        for j, piece in enumerate(pieces)
    ]
    for copy in copies:
        copy.start()
    for copy in copies:
        copy.wait()
    lane = lax.broadcasted_iota(jnp.int32, (1, LANES), 1)

    def step(index, carry):
        block = index // groups
        group = lax.rem(index, groups)
        starts = [((group * GROUP + r) * BLOCKS + block) * SLABS for r in range(GROUP)]
        for s in range(SLABS):
            for r in range(GROUP):
                at = s * span + r * LANES
                current[:, at : at + LANES] = tile[
                    pl.ds(starts[r] + s, members, stride=stride), :
                ]
        lons = (block * LANES + lane).astype(jnp.float32)
        for b in range(NB):
            for s in range(SLABS):
                part = current[:, s * span : (s + 1) * span]
                high, low = split(part - jnp.mean(part, axis=0, keepdims=True))
                spread[:, s * span : (s + 1) * span] = jnp.concatenate([high, low, high], axis=0)
            for chunk in range(CHUNKS):

                @pl.when(near[b, chunk, block] != 0)
                def _():
                    here = pl.ds(chunk * CHUNK, CHUNK)
                    rows_here = obs_row[b, here, :]
                    lons_here = obs_lon[b, here, :]
                    gains = None
                    for s in range(SLABS):
                        if s == 0 or not shared:
                            gains = jnp.concatenate(
                                [
                                    taper_of(
                                        (first_row[s] + group * GROUP + r).astype(jnp.float32),
                                        lons,
                                        rows_here,
                                        lons_here,
                                    )
                                    for r in range(GROUP)
                                ],
                                axis=1,
                            )
                        cov = jnp.dot(
                            anom[b, here, :],
                            spread[:, s * span : (s + 1) * span],
                            preferred_element_type=jnp.float32,
                        )
                        high, low = split(cov * gains)
                        current[:, s * span : (s + 1) * span] += jnp.dot(
                            weight[b, chunk],
                            jnp.concatenate([high, low, high], axis=0),
                            preferred_element_type=jnp.float32,
                        )
        for s in range(SLABS):
            for r in range(GROUP):
                at = s * span + r * LANES
                tile[pl.ds(starts[r] + s, members, stride=stride), :] = current[
                    :, at : at + LANES
                ]
        return carry

    lax.fori_loop(0, BLOCKS * groups, step, 0)
    copies = [
        pltpu.make_async_copy(tile.at[pl.ds(j * piece_rows, piece_rows)], result, sems.at[j])
        for j, result in enumerate(results)
    ]
    for copy in copies:
        copy.start()
    for copy in copies:
        copy.wait()


def update(pieces, near, first_row, anom, weight, obs_row, obs_lon, members, shared):
    mem_n = len(pieces)
    piece_rows = pieces[0].shape[0]
    whole = pl.BlockSpec(memory_space=pltpu.VMEM)
    scalars = pl.BlockSpec(memory_space=pltpu.SMEM)
    hbm = pl.BlockSpec(memory_space=pl.ANY)
    return pl.pallas_call(
        functools.partial(update_kernel, mem_n, members, shared),
        out_shape=[jax.ShapeDtypeStruct(p.shape, jnp.float32) for p in pieces],
        in_specs=[scalars, scalars, whole, whole, whole, whole] + [hbm] * mem_n,
        out_specs=[hbm] * mem_n,
        scratch_shapes=[
            pltpu.VMEM((mem_n * piece_rows, LANES), jnp.float32),
            pltpu.VMEM((members, SLABS * GROUP * LANES), jnp.float32),
            pltpu.VMEM((3 * members, SLABS * GROUP * LANES), jnp.bfloat16),
            pltpu.SemaphoreType.DMA((mem_n,)),
        ],
        compiler_params=pltpu.CompilerParams(vmem_limit_bytes=24 * 1024 * 1024),
        cost_estimate=pl.CostEstimate(flops=2 * 10**10, bytes_accessed=5 * 10**6, transcendentals=0),
        name="update",
    )(near, first_row, anom, weight, obs_row, obs_lon, *pieces)


def by_longitude(columns, arrays):
    lons = columns % NLON
    count = columns.shape[1]
    index = jnp.arange(count, dtype=jnp.int32)
    before = (lons[:, :, None] < lons[:, None, :]) | (
        (lons[:, :, None] == lons[:, None, :]) & (index[:, None] < index[None, :])[None]
    )
    rank = jnp.sum(before.astype(jnp.int32), axis=1)
    chosen = rank[:, :, None] == index[None, None, :]
    return [jnp.sum(jnp.where(chosen, a[:, :, None], jnp.zeros((), a.dtype)), axis=1) for a in arrays]


def near_blocks(columns):
    lons = columns % NLON
    past = (lons[:, :, None] - (jnp.arange(BLOCKS, dtype=jnp.int32) * LANES)[None, None, :]) % NLON
    hit = (past < LANES + REACH) | (past > NLON - REACH)
    hit = jnp.pad(hit, ((0, 0), (0, PADDED - P_SIZE), (0, 0)))
    return jnp.any(hit.reshape(NB, CHUNKS, CHUNK, BLOCKS), axis=2).astype(jnp.int32)


def local(prior, obs_column, obs_level, obs_value, obs_variance):
    own_members, own_levels, all_columns = prior.shape
    mem_n = lax.axis_size("mem")
    col_n = lax.axis_size("col")
    m = lax.axis_index("mem")
    c = lax.axis_index("col")
    members = own_members * mem_n
    parts = SLABS // own_levels
    part_columns = all_columns // parts
    width = part_columns // mem_n
    tiles = part_columns // LANES
    tiles = part_columns // LANES
    prior = prior.reshape(own_members, SLABS, tiles, LANES).transpose(0, 2, 1, 3)
    prior = prior.reshape(own_members, tiles * SLABS, LANES)
    piece = tiles * SLABS // (mem_n * HALVES)
    peers = [jnp.bitwise_xor(m, j) for j in range(mem_n)]
    pairs = [[(i, i ^ j) for i in range(mem_n)] for j in range(mem_n)]

    def swap(parts):
        return [parts[0]] + [lax.ppermute(parts[j], "mem", pairs[j]) for j in range(1, mem_n)]

    def fetch(half):
        return swap(
            [
                lax.dynamic_slice_in_dim(prior, (peer * HALVES + half) * piece, piece, 1)
                for peer in peers
            ]
        )

    arrived = [fetch(0)]

    columns, levels, values, variances = by_longitude(
        obs_column, [obs_column, obs_level, obs_value, obs_variance]
    )

    flat_column = columns.reshape(-1)
    flat_level = levels.reshape(-1)
    slab = (flat_level % own_levels) * parts + flat_column // part_columns
    part_column = flat_column % part_columns
    owned = flat_level // own_levels == c
    row = part_column // LANES * SLABS + slab
    picked = pick(
        prior.reshape(own_members * tiles * SLABS, LANES),
        jnp.where(owned, row, 0),
        part_column % LANES,
        owned.astype(jnp.int32),
        own_members,
    )
    obs = gather(picked, mem_n, col_n)
    for half in range(1, HALVES):
        prior, arrived[half - 1] = lax.optimization_barrier((prior, arrived[half - 1]))
        arrived.append(fetch(half))
    obs = obs[:, :, :own_members]
    obs = jnp.take(obs, jnp.stack(peers), axis=0).transpose(0, 2, 1, 3)
    obs = obs.reshape(members, NB, P_SIZE)

    rows = (columns // NLON).astype(jnp.float32)
    lons = (columns % NLON).astype(jnp.float32)
    scale = 1.0 / (members - 1)
    state = [obs[:, b] for b in range(NB)]
    anoms, weights = [], []
    for b in range(NB):
        obs_anom, weight = obs_weights(state[b], values[b], variances[b])
        anoms.append(obs_anom * scale)
        weights.append(weight)
        for later in range(b + 1, NB):
            anomalies = state[later] - jnp.mean(state[later], axis=0)[None]
            cov = jnp.einsum(
                "kp,kc->pc",
                obs_anom * scale,
                anomalies,
                precision=lax.Precision.HIGHEST,
                preferred_element_type=jnp.float32,
            )
            gain = cov * taper_of(
                rows[later][None, :], lons[later][None, :], rows[b][:, None], lons[b][:, None]
            )
            state[later] = state[later] + jnp.einsum(
                "kp,pc->kc",
                weight,
                gain,
                precision=lax.Precision.HIGHEST,
                preferred_element_type=jnp.float32,
            )

    extra = PADDED - P_SIZE
    high, low = split_outside(jnp.stack(anoms).transpose(0, 2, 1))
    anom = jnp.pad(jnp.concatenate([high, high, low], axis=2), ((0, 0), (0, extra), (0, 0)))
    weight = jnp.pad(jnp.stack(weights), ((0, 0), (0, 0), (0, extra)))
    weight = weight.reshape(NB, members, CHUNKS, CHUNK).transpose(0, 2, 1, 3)
    high, low = split_outside(weight)
    weight = jnp.concatenate([high, high, low], axis=3)
    obs_row = jnp.pad(rows, ((0, 0), (0, extra)))[:, :, None]
    obs_lon = jnp.pad(lons, ((0, 0), (0, extra)))[:, :, None]

    slabs = jnp.arange(SLABS, dtype=jnp.int32)
    near = near_blocks(columns)
    pieces = []
    for half in range(HALVES):
        first_row = (slabs % parts) * part_columns + m * width + half * (width // HALVES)
        done = update(
            [p.reshape(own_members * piece, LANES) for p in arrived[half]],
            near,
            first_row // NLON,
            anom,
            weight,
            obs_row,
            obs_lon,
            members,
            parts == 1,
        )
        pieces += [p.reshape(own_members, piece, LANES) for p in swap(done)]
    out = join(pieces, mem_n).reshape(own_members, tiles, SLABS, LANES)
    out = out.transpose(0, 2, 1, 3)
    return out.reshape(own_members, own_levels, all_columns)


def solution(mesh):
    return jax.shard_map(
        local,
        mesh=mesh,
        in_specs=(P("mem", "col", None), P(), P(), P(), P()),
        out_specs=P("mem", "col", None),
        check_vma=False,
    )
```
